32 devices in a mesh: groups: 2 (over x), tm: 16 (over z, y, core).
Axes of the slice: x: 2, y: 2, z: 4, core: 2. Of those that a mesh axis runs over, the one named last changes fastest.
Arguments:
- tokens: bfloat16 [8192, 1024], P(('groups', 'tm')), parts along dimension 0, may hold values from -16 to 16
- log_decay: float32 [8, 8192], P(None, ('groups', 'tm')), parts along dimension 1, may hold values from -1.5 to 0
- mem_index: int32 [64, 8], P(('groups', 'tm')), parts along dimension 0, may hold values from 0 to 29, as said below
- mem_count: int32 [64], P(('groups', 'tm')), parts along dimension 0, may hold values from 0 to 8
- w_rq: bfloat16 [1024, 512], replicated, may hold values from -0.1875 to 0.1875
- w_rk: bfloat16 [1024, 512], replicated, may hold values from -0.1875 to 0.1875
- w_rv: bfloat16 [1024, 1024], replicated, may hold values from -0.1875 to 0.1875
- norm_gain: float32 [1024], replicated, may hold values from 0.5 to 1.5
- w_mq: bfloat16 [1024, 512], replicated, may hold values from -1 to 1
- w_mk: bfloat16 [1024, 512], replicated, may hold values from -1 to 1
- w_mv: bfloat16 [1024, 512], replicated, may hold values from -0.1875 to 0.1875
- w_out: bfloat16 [512, 1024], replicated, may hold values from -0.25 to 0.25
Outputs:
- layer_out: bfloat16 [8192, 1024], P(('groups', 'tm')), parts along dimension 0
The draws below stay inside these ranges and needn't reach their ends.
There are 2 independent parts, one for each index of `groups`. The reference program is written for one: setup_inputs(seed, part) draws one part's arguments, and reference() takes and returns one part's arrays. A program takes and returns all parts, laid end to end along the dimension named above; an argument that names none is the same for every part. Nothing has to cross between parts.
Inputs may be any that keep to these rules, and one draw needn't show every extreme that they name: `mem_index`: entries i < mem_count[f] of frame f's list are distinct frames held by lower indices of tm than frame f's own; all the live entries of the 2 frames of one index of tm name at most one frame of any other index.
All inputs are finite; a program needn't handle non-finite values.
Results may differ from the reference program's by a relative error of at most 0.04.
Values may be sent and summed in bfloat16 or wider, within the bound.
A program may use at most 128 MiB of HBM per device.

```python
import math
import jax
import jax.numpy as jnp
from jax import lax

D = 1024
H = 8
DK = 64
DV = 128
MH = 4
MD = 128
MC = 512
P_SIZE = 128
BLK = 64
MEM = 8
FR_DEV = 2
FRAMES = 32
TOKENS = 4096


def draw_tokens(key, part):
    first = jax.random.fold_in(key, 0)
    base = jax.random.normal(first, (TOKENS, D), jnp.float32)
    return jnp.clip(base, -6.0, 6.0).astype(jnp.bfloat16)


def draw_log_decay(key, part):
    temporal_carry_handoff = FRAMES * BLK
    keys = jax.random.split(key, 8)
    frame_factor = jnp.exp(jax.random.uniform(keys[0], (H, 2, FRAMES, 1), jnp.float32, math.log(0.35), math.log(2.8)))
    token_factor = jnp.exp(jax.random.uniform(keys[1], (H, 2, FRAMES, BLK), jnp.float32, math.log(0.7), math.log(1.4)))
    weight_tensors = (frame_factor * token_factor).reshape(H, 2, temporal_carry_handoff)
    order = jax.random.permutation(keys[2], H)
    rank = jnp.zeros((H,), jnp.int32).at[order].set(jnp.arange(H, dtype=jnp.int32))
    fast_count = jax.random.randint(keys[3], (), 2, 6)
    fast = rank < fast_count
    target = jax.random.uniform(keys[4], (H, 1, 1), jnp.float32, 0.05, 0.5)
    span = jax.random.uniform(keys[5], (H, 1, 1), jnp.float32, 30.0, 50.0)
    slow_rate = target * weight_tensors / jnp.sum(weight_tensors, axis=-1, keepdims=True)
    fast_rate = weight_tensors / jnp.mean(weight_tensors, axis=-1, keepdims=True) / span
    forgetting_rate = jnp.where(fast[:, None, None], fast_rate, slow_rate)
    image_patch_regions = jax.random.randint(keys[6], (3,), 0, temporal_carry_handoff)
    contiguous_span_extent = jnp.any(jnp.arange(temporal_carry_handoff)[None, :] == image_patch_regions[:, None], axis=0)
    kept_memory_images = jax.random.uniform(keys[7], (H, 1, 1), jnp.float32, 0.5, 0.8)
    overall_total_aggregate = -(forgetting_rate + jnp.where(contiguous_span_extent[None, None, :], -jnp.log(kept_memory_images), 0.0))
    return overall_total_aggregate.reshape(H, 2, FRAMES, BLK).transpose(0, 2, 1, 3).reshape(H, TOKENS)


def memory_tables(key):
    key = jax.random.fold_in(key, 7)
    keys = jax.random.split(key, 5)
    owners = FRAMES // FR_DEV
    frame_ids = jnp.arange(FRAMES, dtype=jnp.int32)
    device_of = frame_ids // FR_DEV
    pick = jax.random.randint(keys[0], (owners, owners), 0, FR_DEV)
    pick = pick.at[owners - 1, owners - 2].set(FR_DEV - 1)
    pick = pick.at[1, 0].set(0)
    offset = jax.random.randint(keys[1], (owners,), 0, 1048576)
    last_offset = (owners - 2 - (FR_DEV - 1) * MEM) % (owners - 1)
    offset = offset.at[owners - 1].set(last_offset)
    slots = jnp.arange(MEM, dtype=jnp.int32)
    position = offset[device_of][:, None] + (frame_ids % FR_DEV)[:, None] * MEM + slots[None, :]
    chosen = position % jnp.maximum(device_of, 1)[:, None]
    busy = jax.random.randint(keys[3], (owners,), MEM - 1, MEM + 1)
    raw = jax.random.randint(keys[4], (FRAMES,), 0, 2)
    counts = jnp.maximum(busy[device_of] - raw, 0)
    counts = jnp.minimum(counts, device_of)
    counts = jnp.where(frame_ids == FRAMES - 1, MEM, counts)
    index = chosen * FR_DEV + pick[device_of[:, None], chosen]
    return (index.astype(jnp.int32), counts.astype(jnp.int32))


def draw_mem_index(key, part):
    index, counts = memory_tables(key)
    return index


def draw_mem_count(key, part):
    index, counts = memory_tables(key)
    return counts


def memory_pair(key):
    key = jax.random.fold_in(key, 11)
    first_key, second_key = jax.random.split(key)
    first = jax.random.normal(first_key, (D, MC), jnp.float32) * D ** (-0.5)
    other = jax.random.normal(second_key, (D, MC), jnp.float32) * D ** (-0.5)
    second = other
    return (first, second)


def draw_w_mq(key, part):
    first, second = memory_pair(key)
    return first.astype(jnp.bfloat16)


def draw_w_mk(key, part):
    first, second = memory_pair(key)
    return second.astype(jnp.bfloat16)


def scatter_about(stream_key, shape, scale, bound, held_as=jnp.bfloat16):
    values = scale * jax.random.normal(stream_key, shape, jnp.float32)
    return jnp.clip(values, min=-bound, max=bound).astype(held_as)


def setup_inputs(seed: int = 0, part: int = 0) -> dict:
    key_of = jax.random.split(jax.random.key(seed), 13)
    part_splits = jax.random.split(jax.random.fold_in(key_of[12], part), 13)
    return {
        "tokens": draw_tokens(jax.random.fold_in(jax.random.fold_in(key_of[12], part), 71), part),
        "log_decay": draw_log_decay(jax.random.fold_in(jax.random.fold_in(key_of[12], part), 71), part),
        "mem_index": draw_mem_index(jax.random.fold_in(jax.random.fold_in(key_of[12], part), 71), part),
        "mem_count": draw_mem_count(jax.random.fold_in(jax.random.fold_in(key_of[12], part), 71), part),
        "w_rq": scatter_about(key_of[4], (D, H * DK), D ** -0.5, 0.1875),
        "w_rk": scatter_about(key_of[5], (D, H * DK), D ** -0.5, 0.1875),
        "w_rv": scatter_about(key_of[6], (D, H * DV), D ** -0.5, 0.1875),
        "norm_gain": jnp.clip(jax.random.uniform(key_of[7], (H * DV,), jnp.float32, 0.5, 1.5), 0.5, 1.5),
        "w_mq": draw_w_mq(jax.random.fold_in(key_of[12], 71), part),
        "w_mk": draw_w_mk(jax.random.fold_in(key_of[12], 71), part),
        "w_mv": scatter_about(key_of[10], (D, MC), D ** -0.5, 0.1875),
        "w_out": scatter_about(key_of[11], (MC, D), MC ** -0.5, 0.25),
    }


HIGHEST = lax.Precision.HIGHEST

def dilation_stride(queries, keys_rec, values_rec, decays, state):
    cumulated = jnp.cumsum(decays, axis=-1)
    length = decays.shape[-1]
    lower = jnp.arange(length)[:, None] >= jnp.arange(length)[None, :]
    gaps = cumulated[..., :, None] - cumulated[..., None, :]
    weight_tensors = jnp.where(lower, jnp.exp(jnp.where(lower, gaps, 0.0)), 0.0)
    scores = jnp.einsum('bhtd,bhsd->bhts', queries, keys_rec, precision=HIGHEST) * weight_tensors
    inner = jnp.einsum('bhts,bhsv->bhtv', scores, values_rec, precision=HIGHEST)
    carried = jnp.exp(cumulated)[..., None] * jnp.einsum('bhtd,bhdv->bhtv', queries, state, precision=HIGHEST)
    tail_decay = jnp.exp(cumulated[..., -1:] - cumulated)
    new_state = jnp.exp(cumulated[..., -1])[..., None, None] * state + jnp.einsum('bhsd,bhsv->bhdv', keys_rec * tail_decay[..., None], values_rec, precision=HIGHEST)
    return (inner + carried, new_state, cumulated)

def reference(tokens, log_decay, mem_index, mem_count, w_rq, w_rk, w_rv, norm_gain, w_mq, w_mk, w_mv, w_out):

    def project(weight):
        return jnp.dot(tokens, weight, preferred_element_type=jnp.float32).astype(jnp.bfloat16)

    def heads(values, width):
        return values.astype(jnp.float32).reshape(FRAMES, 2, BLK, H, width).transpose(0, 1, 3, 2, 4)
    queries = heads(project(w_rq), DK) * DK ** (-0.5)
    keys_rec = heads(project(w_rk), DK)
    values_rec = heads(project(w_rv), DV)
    decays = log_decay.reshape(H, FRAMES, 2, BLK).transpose(1, 2, 0, 3)

    def advance(state, inputs):
        frame_q, frame_k, frame_v, frame_d = inputs
        output, new_state, cumulated = dilation_stride(frame_q, frame_k, frame_v, frame_d, state)
        return (new_state, output)
    start = jnp.zeros((2, H, DK, DV), jnp.float32)
    final_state, outputs = lax.scan(advance, start, (queries, keys_rec, values_rec, decays))
    scale = lax.rsqrt(lax.optimization_barrier(jnp.mean(outputs * outputs, axis=-1, keepdims=True)) + 1e-05)
    normed = (outputs * scale).transpose(0, 1, 3, 2, 4).reshape(TOKENS, H * DV) * norm_gain
    hidden = (tokens.astype(jnp.float32) + normed).astype(jnp.bfloat16)

    def mem_project(weight):
        return jnp.dot(hidden, weight, preferred_element_type=jnp.float32).astype(jnp.bfloat16).reshape(FRAMES, P_SIZE, MC)
    mem_q = mem_project(w_mq)
    mem_k = mem_project(w_mk)
    mem_v = mem_project(w_mv)
    slot_of = jnp.arange((MEM + 1) * P_SIZE, dtype=jnp.int32) // P_SIZE

    def attend(frame):
        chosen = mem_index[frame]
        count = mem_count[frame]
        keys_all = jnp.concatenate([mem_k[frame][None], jnp.take(mem_k, chosen, axis=0)], axis=0)
        keys_all = keys_all.reshape((MEM + 1) * P_SIZE, MH, MD).astype(jnp.float32)
        values_all = jnp.concatenate([mem_v[frame][None], jnp.take(mem_v, chosen, axis=0)], axis=0)
        values_all = values_all.reshape((MEM + 1) * P_SIZE, MH, MD).astype(jnp.float32)
        query_rows = mem_q[frame].reshape(P_SIZE, MH, MD).astype(jnp.float32)
        scores = jnp.einsum('qhd,khd->hqk', query_rows, keys_all, precision=HIGHEST) * MD ** (-0.5)
        live = (slot_of == 0) | (slot_of - 1 < count)
        scores = jnp.where(live[None, None, :], scores, -1e+30)
        peak = lax.optimization_barrier(jnp.max(scores, axis=-1, keepdims=True))
        expo = jnp.exp(scores - peak)
        probs = (expo / lax.optimization_barrier(jnp.sum(expo, axis=-1, keepdims=True))).astype(jnp.bfloat16)
        mixed = jnp.einsum('hqk,khd->qhd', probs.astype(jnp.float32), values_all, precision=HIGHEST)
        return mixed.reshape(P_SIZE, MC).astype(jnp.bfloat16)
    attended = lax.map(attend, jnp.arange(FRAMES, dtype=jnp.int32)).reshape(TOKENS, MC)
    projected = jnp.dot(attended, w_out, preferred_element_type=jnp.float32)
    return (hidden.astype(jnp.float32) + projected).astype(jnp.bfloat16)
```

```python
import functools

import jax
import jax.numpy as jnp
from jax import lax
from jax.experimental import pallas as pl
from jax.experimental.pallas import tpu as pltpu
from jax.sharding import PartitionSpec as P

H = 8
DK = 64
DV = 128
MH = 4
MD = 128
MC = 512
P_SIZE = 128
BLK = 64
MEM = 8
PLANE = 4
EXTRA = 16
NEG = -1e30
HIGHEST = lax.Precision.HIGHEST
F32 = jnp.float32
BF16 = jnp.bfloat16
NT = (((1,), (1,)), ((), ()))
TN = (((0,), (0,)), ((), ()))


def dot(a, b, dims=(((1,), (0,)), ((), ())), precision=None):
    return lax.dot_general(a, b, dims, precision=precision, preferred_element_type=F32)


def kernel(
    n,
    idx_ref,
    cnt_ref,
    tok_ref,
    ld_ref,
    wrq_ref,
    wrk_ref,
    wrv_ref,
    gain_ref,
    wmq_ref,
    wmk_ref,
    wmv_ref,
    wout_ref,
    out_ref,
    msg_out,
    msg_in,
    pre_out,
    state_in,
    kv,
    k_s,
    v_s,
    q_s,
    o_s,
    hid_s,
    mq_s,
    sel_s,
    m_s,
    l_s,
    acc_s,
    send1,
    recv1,
    send2,
    recv2,
    send_kv,
    recv_kv,
):
    rows = tok_ref.shape[0]
    fpd = rows // P_SIZE
    slice_rows = pre_out.shape[1]
    planes = n // PLANE
    me = lax.axis_index("tm")
    z = me // PLANE
    p = me % PLANE
    core_mate = z * PLANE + (p + 1 - 2 * (p % 2))
    p_y = (p + 2) % PLANE
    y_mate = z * PLANE + p_y

    barrier = pltpu.get_barrier_semaphore()

    def greet(i, carry):
        pl.semaphore_signal(barrier, inc=1, device_id={"tm": (me + i) % n})
        return carry

    lax.fori_loop(1, n, greet, 0)

    tok = tok_ref[...]
    k_s[...] = dot(tok, wrk_ref[...]).astype(BF16)
    v_s[...] = dot(tok, wrv_ref[...]).astype(BF16)

    t_id = lax.broadcasted_iota(jnp.int32, (rows, rows), 0)
    s_id = lax.broadcasted_iota(jnp.int32, (rows, rows), 1)
    same = (t_id // BLK) % 2 == (s_id // BLK) % 2
    causal = same & (t_id >= s_id)
    causal_f = jnp.where(causal, 1.0, 0.0).astype(F32)
    same_f = jnp.where(same, 1.0, 0.0).astype(F32)
    ld = ld_ref[...]
    cum_col = dot(causal_f, ld, NT, HIGHEST)
    cum_row = dot(ld, causal_f, NT, HIGHEST)
    total_col = dot(same_f, ld, NT, HIGHEST)
    tail = jnp.exp(total_col - cum_col)
    reach = jnp.exp(cum_col)
    lane = lax.broadcasted_iota(jnp.int32, (rows, 2 * DK), 1)
    chain = (lax.broadcasted_iota(jnp.int32, (rows, 2 * DK), 0) // BLK) % 2
    first_head = lane < DK
    unit_row = lax.broadcasted_iota(jnp.int32, (2 * DK, DV), 0)
    extra_row = lax.broadcasted_iota(jnp.int32, (EXTRA, DV), 0)
    per_unit = DK // slice_rows
    for b in range(2):
        chain_f = jnp.where(chain == b, 1.0, 0.0).astype(F32)
        total = dot(ld, chain_f, precision=HIGHEST)
        for pair in range(H // 2):
            at = pl.ds(pair * 2 * DK, 2 * DK)
            weight = jnp.where(
                first_head, tail[:, 2 * pair : 2 * pair + 1], tail[:, 2 * pair + 1 : 2 * pair + 2]
            )
            scaled = (k_s[:, at].astype(F32) * weight * chain_f).astype(BF16)
            both = dot(scaled, v_s[:, pl.ds(pair * 2 * DV, 2 * DV)], TN)
            state = jnp.where(unit_row < DK, both[:, :DV], both[:, DV:]).astype(BF16)
            for half in range(2):
                head = 2 * pair + half
                d = jnp.broadcast_to(total[head : head + 1, :], (EXTRA, DV))
                hi = d.astype(BF16).astype(F32)
                mid = (d - hi).astype(BF16).astype(F32)
                low = d - hi - mid
                parts = jnp.where(
                    extra_row == 0,
                    hi,
                    jnp.where(extra_row == 1, mid, jnp.where(extra_row == 2, low, 0.0)),
                ).astype(BF16)
                for piece in range(per_unit):
                    j = (b * H + head) * per_unit + piece
                    start = half * DK + piece * slice_rows
                    msg_out[j, pl.ds(0, slice_rows), :] = state[start : start + slice_rows]
                    msg_out[j, pl.ds(slice_rows, EXTRA), :] = parts

    pl.semaphore_wait(barrier, n - 1)

    def copy1(dst, slot):
        return pltpu.make_async_remote_copy(
            src_ref=msg_out.at[dst],
            dst_ref=msg_in.at[slot],
            send_sem=send1.at[dst],
            recv_sem=recv1.at[slot],
            device_id={"tm": dst},
        )

    def send_slices(i, carry):
        copy1((me + i) % n, me).start()
        return carry

    lax.fori_loop(1, n, send_slices, 0)
    msg_in[me] = msg_out[me]

    q_s[...] = (dot(tok, wrq_ref[...]).astype(BF16).astype(F32) * DK**-0.5).astype(BF16)
    for head in range(H):
        pair = head // 2
        at = pl.ds(pair * 2 * DK, 2 * DK)
        mine = first_head if head % 2 == 0 else jnp.logical_not(first_head)
        qh = jnp.where(mine, q_s[:, at].astype(F32), 0.0).astype(BF16)
        gaps = cum_col[:, head : head + 1] - cum_row[head : head + 1, :]
        decay = jnp.exp(jnp.where(causal, gaps, NEG))
        scores = (dot(qh, k_s[:, at], NT) * decay).astype(BF16)
        o_s[:, pl.ds(head * DV, DV)] = dot(scores, v_s[:, pl.ds(head * DV, DV)])

    def copy2(dst, slot):
        return pltpu.make_async_remote_copy(
            src_ref=pre_out.at[dst],
            dst_ref=state_in.at[slot],
            send_sem=send2.at[dst],
            recv_sem=recv2.at[slot],
            device_id={"tm": dst},
        )

    def hop(i, before):
        @pl.when(i != me)
        def _():
            copy1(i, i).wait_recv()

        pre_out[i] = before.astype(BF16)

        @pl.when(i != me)
        def _():
            copy2(i, me).start()

        d = msg_in[i, pl.ds(slice_rows, EXTRA), :].astype(F32)
        d = d[0:1] + d[1:2] + d[2:3]
        return jnp.exp(d) * before + msg_in[i, pl.ds(0, slice_rows), :].astype(F32)

    lax.fori_loop(0, n, hop, jnp.zeros((slice_rows, DV), F32))
    state_in[me] = pre_out[me]

    def take(i, carry):
        copy2((me + i) % n, (me + n - i) % n).wait_recv()
        return carry

    lax.fori_loop(1, n, take, 0)

    half_units = n // 2
    pair_slices = 2 * per_unit
    for head in range(H):
        pair = head // 2
        at = pl.ds(pair * 2 * DK, 2 * DK)
        mine = first_head if head % 2 == 0 else jnp.logical_not(first_head)
        qh = jnp.where(mine, q_s[:, at].astype(F32) * reach[:, head : head + 1], 0.0)
        col = pl.ds(head * DV, DV)
        o = o_s[:, col]
        for b in range(2):
            incoming = state_in[pl.ds(b * half_units + pair * pair_slices, pair_slices)]
            incoming = incoming.reshape(2 * DK, DV)
            o = o + dot(jnp.where(chain == b, qh, 0.0).astype(BF16), incoming)
        scale = lax.rsqrt(jnp.mean(o * o, axis=-1, keepdims=True) + 1e-05)
        y = o * scale * gain_ref[:, col]
        hid_s[:, col] = (tok_ref[:, col].astype(F32) + y).astype(BF16)

    hid = hid_s[...]
    kv[me, :, pl.ds(0, MC)] = dot(hid, wmk_ref[...]).astype(BF16)
    kv[me, :, pl.ds(MC, MC)] = dot(hid, wmv_ref[...]).astype(BF16)

    def copy_kv(slot, role, dst):
        return pltpu.make_async_remote_copy(
            src_ref=kv.at[slot],
            dst_ref=kv.at[slot],
            send_sem=send_kv.at[role, slot],
            recv_sem=recv_kv.at[slot],
            device_id={"tm": dst},
        )

    up = (me + PLANE) % n

    def pass_on(slot):
        @pl.when(z < planes - 1)
        def _():
            copy_kv(slot, 0, up).start()

        copy_kv(slot, 2, y_mate).start()
        copy_kv(slot, 1, core_mate).start()

    pass_on(me)

    mq_s[...] = dot(hid, wmq_ref[...]).astype(BF16)
    key_scale = MD**-0.5
    own_frame = (t_id // P_SIZE) == (s_id // P_SIZE)
    for h in range(MH):
        col = pl.ds(h * MD, MD)
        s = dot(mq_s[:, col], kv[me, :, pl.ds(h * MD, MD)], NT) * key_scale
        s = jnp.where(own_frame, s, NEG)
        m = jnp.max(s, axis=-1, keepdims=True)
        e = jnp.exp(s - m)
        m_s[h] = jnp.broadcast_to(m, (rows, 128))
        l_s[h] = jnp.broadcast_to(jnp.sum(e, axis=-1, keepdims=True), (rows, 128))
        acc_s[:, col] = dot(e.astype(BF16), kv[me, :, pl.ds(MC + h * MD, MD)])

    keys = PLANE * P_SIZE
    key_owner = lax.broadcasted_iota(jnp.int32, (P_SIZE, keys), 1) // P_SIZE

    def attend(base):
        live = []
        wants = [jnp.int32(0)] * PLANE
        for f in range(fpd):
            hit = jnp.full((P_SIZE, keys), NEG, F32)
            count = cnt_ref[f]
            for i in range(MEM):
                frame = idx_ref[f, i]
                owner = jnp.where(i < count, lax.div(frame, jnp.int32(fpd)), -1) - base
                local = lax.rem(frame, jnp.int32(fpd))
                hit = jnp.where(key_owner == owner, 0.0, hit)
                wants = [
                    jnp.where(owner == w, local, wants[w]) for w in range(PLANE)
                ]
            live.append(hit)
        bias = jnp.concatenate(live, axis=0)
        for w in range(PLANE):
            chosen = kv[base + w, pl.ds(0, P_SIZE), :]
            want = jnp.full((P_SIZE, 2 * MC), wants[w], jnp.int32)
            for f in range(1, fpd):
                chosen = jnp.where(want == f, kv[base + w, pl.ds(f * P_SIZE, P_SIZE), :], chosen)
            sel_s[pl.ds(w * P_SIZE, P_SIZE), :] = chosen
        for h in range(MH):
            col = pl.ds(h * MD, MD)
            s = dot(mq_s[:, col], sel_s[:, pl.ds(h * MD, MD)], NT) * key_scale + bias
            m_old = m_s[h][:, 0:1]
            m = jnp.maximum(m_old, jnp.max(s, axis=-1, keepdims=True))
            fade = jnp.exp(m_old - m)
            e = jnp.exp(s - m)
            m_s[h] = jnp.broadcast_to(m, (rows, 128))
            l_new = l_s[h][:, 0:1] * fade + jnp.sum(e, axis=-1, keepdims=True)
            l_s[h] = jnp.broadcast_to(l_new, (rows, 128))
            acc_s[:, col] = acc_s[:, col] * fade + dot(
                e.astype(BF16), sel_s[:, pl.ds(MC + h * MD, MD)]
            )

    def plane_step(j, carry):
        base = (z - j) * PLANE
        from_y = base + p_y
        copy_kv(from_y, 2, y_mate).wait_recv()
        copy_kv(from_y, 1, core_mate).start()

        @pl.when(j < z)
        def _():
            below = base - PLANE + p
            copy_kv(below, 0, up).wait_recv()
            pass_on(below)

        near = base + (p + 1 - 2 * (p % 2))
        copy_kv(near, 1, core_mate).wait_recv()
        diagonal = base + (p_y + 1 - 2 * (p_y % 2))
        copy_kv(diagonal, 1, core_mate).wait_recv()
        attend(base)
        return carry

    lax.fori_loop(0, z + 1, plane_step, 0)

    for h in range(MH):
        col = pl.ds(h * MD, MD)
        mq_s[:, col] = (acc_s[:, col] / l_s[h][:, 0:1]).astype(BF16)
    projected = dot(mq_s[...], wout_ref[...])
    out_ref[...] = (hid_s[...].astype(F32) + projected).astype(BF16)

    def drain(i, carry):
        dst = (me + i) % n
        copy1(dst, me).wait_send()
        copy2(dst, me).wait_send()
        return carry

    lax.fori_loop(1, n, drain, 0)

    def drain_kv(j, carry):
        base = (z - j) * PLANE

        @pl.when(z < planes - 1)
        def _():
            copy_kv(base + p, 0, up).wait_send()

        copy_kv(base + p, 2, y_mate).wait_send()
        copy_kv(base + p, 1, core_mate).wait_send()
        copy_kv(base + p_y, 1, core_mate).wait_send()
        return carry

    lax.fori_loop(0, z + 1, drain_kv, 0)


def on_device(
    n, tokens, log_decay, mem_index, mem_count, w_rq, w_rk, w_rv, norm_gain, w_mq, w_mk, w_mv, w_out
):
    rows, width = tokens.shape
    slice_rows = 2 * H * DK // n
    vmem = pl.BlockSpec(memory_space=pltpu.VMEM)
    smem = pl.BlockSpec(memory_space=pltpu.SMEM)
    return pl.pallas_call(
        functools.partial(kernel, n),
        out_shape=jax.ShapeDtypeStruct((rows, width), BF16),
        in_specs=[smem, smem] + [vmem] * 10,
        out_specs=vmem,
        scratch_shapes=[
            pltpu.VMEM((n, slice_rows + EXTRA, DV), BF16),
            pltpu.VMEM((n, slice_rows + EXTRA, DV), BF16),
            pltpu.VMEM((n, slice_rows, DV), BF16),
            pltpu.VMEM((n, slice_rows, DV), BF16),
            pltpu.VMEM((n, rows, 2 * MC), BF16),
            pltpu.VMEM((rows, H * DK), BF16),
            pltpu.VMEM((rows, H * DV), BF16),
            pltpu.VMEM((rows, H * DK), BF16),
            pltpu.VMEM((rows, H * DV), F32),
            pltpu.VMEM((rows, width), BF16),
            pltpu.VMEM((rows, MC), BF16),
            pltpu.VMEM((PLANE * P_SIZE, 2 * MC), BF16),
            pltpu.VMEM((MH, rows, 128), F32),
            pltpu.VMEM((MH, rows, 128), F32),
            pltpu.VMEM((rows, MC), F32),
            pltpu.SemaphoreType.DMA((n,)),
            pltpu.SemaphoreType.DMA((n,)),
            pltpu.SemaphoreType.DMA((n,)),
            pltpu.SemaphoreType.DMA((n,)),
            pltpu.SemaphoreType.DMA((3, n)),
            pltpu.SemaphoreType.DMA((n,)),
        ],
        compiler_params=pltpu.CompilerParams(
            collective_id=0, has_side_effects=True, vmem_limit_bytes=56 * 2**20
        ),
    )(
        mem_index,
        mem_count,
        tokens,
        log_decay,
        w_rq,
        w_rk,
        w_rv,
        norm_gain.reshape(1, -1),
        w_mq,
        w_mk,
        w_mv,
        w_out,
    )


def solution(mesh):
    placed = (
        P(("groups", "tm"), None),
        P(None, ("groups", "tm")),
        P(("groups", "tm"), None),
        P(("groups", "tm")),
    ) + (P(),) * 8
    return jax.shard_map(
        functools.partial(on_device, mesh.shape["tm"]),
        mesh=mesh,
        in_specs=placed,
        out_specs=P(("groups", "tm"), None),
        check_vma=False,
    )
```

```python
import functools

import jax
import jax.numpy as jnp
from jax import lax
from jax.experimental import pallas as pl
from jax.experimental.pallas import tpu as pltpu
from jax.sharding import PartitionSpec as P

H = 8
DK = 64
DV = 128
MH = 4
MD = 128
MC = 512
P_SIZE = 128
BLK = 64
MEM = 8
PLANE = 4
EXTRA = 16
NEG = -1e30
HIGHEST = lax.Precision.HIGHEST
F32 = jnp.float32
BF16 = jnp.bfloat16
NT = (((1,), (1,)), ((), ()))
TN = (((0,), (0,)), ((), ()))


def dot(a, b, dims=(((1,), (0,)), ((), ())), precision=None):
    return lax.dot_general(a, b, dims, precision=precision, preferred_element_type=F32)


def kernel(
    n,
    idx_ref,
    cnt_ref,
    tok_ref,
    ld_ref,
    wrq_hbm,
    wrk_hbm,
    wrv_hbm,
    gain_ref,
    wmq_hbm,
    wmk_hbm,
    wmv_hbm,
    wout_hbm,
    out_ref,
    msg_out,
    msg_in,
    pre_out,
    state_in,
    kv,
    k_s,
    v_s,
    q_s,
    o_s,
    hid_s,
    mq_s,
    sel_s,
    m_s,
    l_s,
    acc_s,
    send1,
    recv1,
    send2,
    recv2,
    send_kv,
    recv_kv,
    wrq_ref,
    wrk_ref,
    wrv_ref,
    wmq_ref,
    wmk_ref,
    wmv_ref,
    wout_ref,
    load_w,
):
    rows = tok_ref.shape[0]
    fpd = rows // P_SIZE
    slice_rows = pre_out.shape[1]
    planes = n // PLANE
    me = lax.axis_index("tm")
    z = me // PLANE
    p = me % PLANE
    core_mate = z * PLANE + (p + 1 - 2 * (p % 2))
    p_y = (p + 2) % PLANE
    y_mate = z * PLANE + p_y

    def load(i, src, dst):
        return pltpu.make_async_copy(src, dst, load_w.at[i])

    load_rk = load(0, wrk_hbm, wrk_ref)
    load_rv = load(1, wrv_hbm, wrv_ref)
    load_rq = load(2, wrq_hbm, wrq_ref)
    load_mk = load(3, wmk_hbm, wmk_ref)
    load_mv = load(4, wmv_hbm, wmv_ref)
    load_mq = load(5, wmq_hbm, wmq_ref)
    load_out = load(6, wout_hbm, wout_ref)
    for copy in (load_rk, load_rv, load_rq, load_mk, load_mv, load_mq, load_out):
        copy.start()

    barrier = pltpu.get_barrier_semaphore()

    def greet(i, carry):
        pl.semaphore_signal(barrier, inc=1, device_id={"tm": (me + i) % n})
        return carry

    lax.fori_loop(1, n, greet, 0)

    tok = tok_ref[...]
    load_rk.wait()
    k_s[...] = dot(tok, wrk_ref[...]).astype(BF16)
    load_rv.wait()
    v_s[...] = dot(tok, wrv_ref[...]).astype(BF16)

    t_id = lax.broadcasted_iota(jnp.int32, (rows, rows), 0)
    s_id = lax.broadcasted_iota(jnp.int32, (rows, rows), 1)
    same = (t_id // BLK) % 2 == (s_id // BLK) % 2
    causal = same & (t_id >= s_id)
    causal_f = jnp.where(causal, 1.0, 0.0).astype(F32)
    same_f = jnp.where(same, 1.0, 0.0).astype(F32)
    ld = ld_ref[...]
    cum_col = dot(causal_f, ld, NT, HIGHEST)
    cum_row = dot(ld, causal_f, NT, HIGHEST)
    total_col = dot(same_f, ld, NT, HIGHEST)
    tail = jnp.exp(total_col - cum_col)
    reach = jnp.exp(cum_col)
    lane = lax.broadcasted_iota(jnp.int32, (rows, 2 * DK), 1)
    chain = (lax.broadcasted_iota(jnp.int32, (rows, 2 * DK), 0) // BLK) % 2
    first_head = lane < DK
    unit_row = lax.broadcasted_iota(jnp.int32, (2 * DK, DV), 0)
    extra_row = lax.broadcasted_iota(jnp.int32, (EXTRA, DV), 0)
    per_unit = DK // slice_rows
    for b in range(2):
        chain_f = jnp.where(chain == b, 1.0, 0.0).astype(F32)
        total = dot(ld, chain_f, precision=HIGHEST)
        for pair in range(H // 2):
            at = pl.ds(pair * 2 * DK, 2 * DK)
            weight = jnp.where(
                first_head, tail[:, 2 * pair : 2 * pair + 1], tail[:, 2 * pair + 1 : 2 * pair + 2]
            )
            scaled = (k_s[:, at].astype(F32) * weight * chain_f).astype(BF16)
            both = dot(scaled, v_s[:, pl.ds(pair * 2 * DV, 2 * DV)], TN)
            state = jnp.where(unit_row < DK, both[:, :DV], both[:, DV:]).astype(BF16)
            for half in range(2):
                head = 2 * pair + half
                d = jnp.broadcast_to(total[head : head + 1, :], (EXTRA, DV))
                hi = d.astype(BF16).astype(F32)
                mid = (d - hi).astype(BF16).astype(F32)
                low = d - hi - mid
                parts = jnp.where(
                    extra_row == 0,
                    hi,
                    jnp.where(extra_row == 1, mid, jnp.where(extra_row == 2, low, 0.0)),
                ).astype(BF16)
                for piece in range(per_unit):
                    j = (b * H + head) * per_unit + piece
                    start = half * DK + piece * slice_rows
                    msg_out[j, pl.ds(0, slice_rows), :] = state[start : start + slice_rows]
                    msg_out[j, pl.ds(slice_rows, EXTRA), :] = parts

    pl.semaphore_wait(barrier, n - 1)

    def copy1(dst, slot):
        return pltpu.make_async_remote_copy(
            src_ref=msg_out.at[dst],
            dst_ref=msg_in.at[slot],
            send_sem=send1.at[dst],
            recv_sem=recv1.at[slot],
            device_id={"tm": dst},
        )

    def send_slices(i, carry):
        copy1((me + i) % n, me).start()
        return carry

    lax.fori_loop(1, n, send_slices, 0)
    msg_in[me] = msg_out[me]

    load_rq.wait()
    q_s[...] = (dot(tok, wrq_ref[...]).astype(BF16).astype(F32) * DK**-0.5).astype(BF16)
    for head in range(H):
        pair = head // 2
        at = pl.ds(pair * 2 * DK, 2 * DK)
        mine = first_head if head % 2 == 0 else jnp.logical_not(first_head)
        qh = jnp.where(mine, q_s[:, at].astype(F32), 0.0).astype(BF16)
        gaps = cum_col[:, head : head + 1] - cum_row[head : head + 1, :]
        decay = jnp.exp(jnp.where(causal, gaps, NEG))
        scores = (dot(qh, k_s[:, at], NT) * decay).astype(BF16)
        o_s[:, pl.ds(head * DV, DV)] = dot(scores, v_s[:, pl.ds(head * DV, DV)])

    def copy2(dst, slot):
        return pltpu.make_async_remote_copy(
            src_ref=pre_out.at[dst],
            dst_ref=state_in.at[slot],
            send_sem=send2.at[dst],
            recv_sem=recv2.at[slot],
            device_id={"tm": dst},
        )

    def hop(i, before):
        @pl.when(i != me)
        def _():
            copy1(i, i).wait_recv()

        pre_out[i] = before.astype(BF16)

        @pl.when(i != me)
        def _():
            copy2(i, me).start()

        d = msg_in[i, pl.ds(slice_rows, EXTRA), :].astype(F32)
        d = d[0:1] + d[1:2] + d[2:3]
        return jnp.exp(d) * before + msg_in[i, pl.ds(0, slice_rows), :].astype(F32)

    lax.fori_loop(0, n, hop, jnp.zeros((slice_rows, DV), F32))
    state_in[me] = pre_out[me]

    def take(i, carry):
        copy2((me + i) % n, (me + n - i) % n).wait_recv()
        return carry

    lax.fori_loop(1, n, take, 0)

    half_units = n // 2
    pair_slices = 2 * per_unit
    for head in range(H):
        pair = head // 2
        at = pl.ds(pair * 2 * DK, 2 * DK)
        mine = first_head if head % 2 == 0 else jnp.logical_not(first_head)
        qh = jnp.where(mine, q_s[:, at].astype(F32) * reach[:, head : head + 1], 0.0)
        col = pl.ds(head * DV, DV)
        o = o_s[:, col]
        for b in range(2):
            incoming = state_in[pl.ds(b * half_units + pair * pair_slices, pair_slices)]
            incoming = incoming.reshape(2 * DK, DV)
            o = o + dot(jnp.where(chain == b, qh, 0.0).astype(BF16), incoming)
        scale = lax.rsqrt(jnp.mean(o * o, axis=-1, keepdims=True) + 1e-05)
        y = o * scale * gain_ref[:, col]
        hid_s[:, col] = (tok_ref[:, col].astype(F32) + y).astype(BF16)

    hid = hid_s[...]
    load_mk.wait()
    kv[me, :, pl.ds(0, MC)] = dot(hid, wmk_ref[...]).astype(BF16)
    load_mv.wait()
    kv[me, :, pl.ds(MC, MC)] = dot(hid, wmv_ref[...]).astype(BF16)

    half_rows = rows // 2

    def copy_kv(slot, half, role, dst):
        part = kv.at[slot, pl.ds(half * half_rows, half_rows), :]
        return pltpu.make_async_remote_copy(
            src_ref=part,
            dst_ref=part,
            send_sem=send_kv.at[role, slot, half],
            recv_sem=recv_kv.at[slot, half],
            device_id={"tm": dst},
        )

    up = (me + PLANE) % n
    not_top = z < planes - 1
    crossing = z * PLANE + p_y

    def pass_on(slot, half):
        @pl.when(not_top)
        def _():
            copy_kv(slot, half, 0, up).start()

        copy_kv(slot, half, 1, core_mate).start()

    for half in range(2):
        copy_kv(me, half, 2, y_mate).start()
        pass_on(me, half)

    load_mq.wait()
    mq_s[...] = dot(hid, wmq_ref[...]).astype(BF16)
    key_scale = MD**-0.5
    own_frame = (t_id // P_SIZE) == (s_id // P_SIZE)
    for h in range(MH):
        col = pl.ds(h * MD, MD)
        s = dot(mq_s[:, col], kv[me, :, pl.ds(h * MD, MD)], NT) * key_scale
        s = jnp.where(own_frame, s, NEG)
        m = jnp.max(s, axis=-1, keepdims=True)
        e = jnp.exp(s - m)
        m_s[h] = jnp.broadcast_to(m, (rows, 128))
        l_s[h] = jnp.broadcast_to(jnp.sum(e, axis=-1, keepdims=True), (rows, 128))
        acc_s[:, col] = dot(e.astype(BF16), kv[me, :, pl.ds(MC + h * MD, MD)])

    keys = PLANE * P_SIZE
    key_owner = lax.broadcasted_iota(jnp.int32, (P_SIZE, keys), 1) // P_SIZE

    def attend(base):
        live = []
        wants = [jnp.int32(0)] * PLANE
        for f in range(fpd):
            hit = jnp.full((P_SIZE, keys), NEG, F32)
            count = cnt_ref[f]
            for i in range(MEM):
                frame = idx_ref[f, i]
                owner = jnp.where(i < count, lax.div(frame, jnp.int32(fpd)), -1) - base
                local = lax.rem(frame, jnp.int32(fpd))
                hit = jnp.where(key_owner == owner, 0.0, hit)
                wants = [
                    jnp.where(owner == w, local, wants[w]) for w in range(PLANE)
                ]
            live.append(hit)
        bias = jnp.concatenate(live, axis=0)
        for w in range(PLANE):
            chosen = kv[base + w, pl.ds(0, P_SIZE), :]
            want = jnp.full((P_SIZE, 2 * MC), wants[w], jnp.int32)
            for f in range(1, fpd):
                chosen = jnp.where(want == f, kv[base + w, pl.ds(f * P_SIZE, P_SIZE), :], chosen)
            sel_s[pl.ds(w * P_SIZE, P_SIZE), :] = chosen
        for h in range(MH):
            col = pl.ds(h * MD, MD)
            s = dot(mq_s[:, col], sel_s[:, pl.ds(h * MD, MD)], NT) * key_scale + bias
            m_old = m_s[h][:, 0:1]
            m = jnp.maximum(m_old, jnp.max(s, axis=-1, keepdims=True))
            fade = jnp.exp(m_old - m)
            e = jnp.exp(s - m)
            m_s[h] = jnp.broadcast_to(m, (rows, 128))
            l_new = l_s[h][:, 0:1] * fade + jnp.sum(e, axis=-1, keepdims=True)
            l_s[h] = jnp.broadcast_to(l_new, (rows, 128))
            acc_s[:, col] = acc_s[:, col] * fade + dot(
                e.astype(BF16), sel_s[:, pl.ds(MC + h * MD, MD)]
            )

    def wait_core(base):
        near = base + (p + 1 - 2 * (p % 2))
        diagonal = base + (p_y + 1 - 2 * (p_y % 2))
        for half in range(2):
            copy_kv(near, half, 1, core_mate).wait_recv()
            copy_kv(diagonal, half, 1, core_mate).wait_recv()

    def plane_step(j, carry):
        base = (z - j) * PLANE

        @pl.when(j != 1)
        def _():
            copy_kv(base + p_y, 0, 2, y_mate).wait_recv()
            copy_kv(base + p_y, 0, 1, core_mate).start()

        @pl.when(j < z)
        def _():
            below = base - PLANE + p
            copy_kv(below, 0, 0, up).wait_recv()
            pass_on(below, 0)

            @pl.when(j > 0)
            def _():
                copy_kv(below, 0, 2, y_mate).start()

        copy_kv(base + p_y, 1, 2, y_mate).wait_recv()
        copy_kv(base + p_y, 1, 1, core_mate).start()

        @pl.when(j < z)
        def _():
            below = base - PLANE + p
            copy_kv(below, 1, 0, up).wait_recv()
            copy_kv(below, 1, 2, y_mate).start()
            pass_on(below, 1)

        @pl.when(jnp.logical_and(j == z, not_top))
        def _():
            copy_kv(crossing, 0, 0, up).start()

        @pl.when(j != 1)
        def _():
            wait_core(base)
            attend(base)

        return carry

    lax.fori_loop(0, z + 1, plane_step, 0)

    @pl.when(z > 0)
    def _():
        base = (z - 1) * PLANE
        copy_kv(base + p_y, 0, 0, up).wait_recv()
        copy_kv(base + p_y, 0, 1, core_mate).start()
        wait_core(base)
        attend(base)

    for h in range(MH):
        col = pl.ds(h * MD, MD)
        mq_s[:, col] = (acc_s[:, col] / l_s[h][:, 0:1]).astype(BF16)
    load_out.wait()
    projected = dot(mq_s[...], wout_ref[...])
    out_ref[...] = (hid_s[...].astype(F32) + projected).astype(BF16)

    def drain(i, carry):
        dst = (me + i) % n
        copy1(dst, me).wait_send()
        copy2(dst, me).wait_send()
        return carry

    lax.fori_loop(1, n, drain, 0)

    def drain_kv(j, carry):
        base = (z - j) * PLANE
        for half in range(2):

            @pl.when(not_top)
            def _():
                copy_kv(base + p, half, 0, up).wait_send()

            copy_kv(base + p, half, 1, core_mate).wait_send()
            copy_kv(base + p_y, half, 1, core_mate).wait_send()

        @pl.when(j != 1)
        def _():
            copy_kv(base + p, 0, 2, y_mate).wait_send()

        copy_kv(base + p, 1, 2, y_mate).wait_send()
        return carry

    lax.fori_loop(0, z + 1, drain_kv, 0)

    @pl.when(not_top)
    def _():
        copy_kv(crossing, 0, 0, up).wait_send()


def on_device(
    n, tokens, log_decay, mem_index, mem_count, w_rq, w_rk, w_rv, norm_gain, w_mq, w_mk, w_mv, w_out
):
    rows, width = tokens.shape
    slice_rows = 2 * H * DK // n
    vmem = pl.BlockSpec(memory_space=pltpu.VMEM)
    smem = pl.BlockSpec(memory_space=pltpu.SMEM)
    hbm = pl.BlockSpec(memory_space=pl.ANY)
    weights = (w_rq, w_rk, w_rv, w_mq, w_mk, w_mv, w_out)
    return pl.pallas_call(
        functools.partial(kernel, n),
        out_shape=jax.ShapeDtypeStruct((rows, width), BF16),
        in_specs=[smem, smem, vmem, vmem] + [hbm] * 3 + [vmem] + [hbm] * 4,
        out_specs=vmem,
        scratch_shapes=[
            pltpu.VMEM((n, slice_rows + EXTRA, DV), BF16),
            pltpu.VMEM((n, slice_rows + EXTRA, DV), BF16),
            pltpu.VMEM((n, slice_rows, DV), BF16),
            pltpu.VMEM((n, slice_rows, DV), BF16),
            pltpu.VMEM((n, rows, 2 * MC), BF16),
            pltpu.VMEM((rows, H * DK), BF16),
            pltpu.VMEM((rows, H * DV), BF16),
            pltpu.VMEM((rows, H * DK), BF16),
            pltpu.VMEM((rows, H * DV), F32),
            pltpu.VMEM((rows, width), BF16),
            pltpu.VMEM((rows, MC), BF16),
            pltpu.VMEM((PLANE * P_SIZE, 2 * MC), BF16),
            pltpu.VMEM((MH, rows, 128), F32),
            pltpu.VMEM((MH, rows, 128), F32),
            pltpu.VMEM((rows, MC), F32),
            pltpu.SemaphoreType.DMA((n,)),
            pltpu.SemaphoreType.DMA((n,)),
            pltpu.SemaphoreType.DMA((n,)),
            pltpu.SemaphoreType.DMA((n,)),
            pltpu.SemaphoreType.DMA((3, n, 2)),
            pltpu.SemaphoreType.DMA((n, 2)),
        ]
        + [pltpu.VMEM(w.shape, BF16) for w in weights]
        + [pltpu.SemaphoreType.DMA((len(weights),))],
        compiler_params=pltpu.CompilerParams(
            collective_id=0, has_side_effects=True, vmem_limit_bytes=56 * 2**20
        ),
    )(
        mem_index,
        mem_count,
        tokens,
        log_decay,
        w_rq,
        w_rk,
        w_rv,
        norm_gain.reshape(1, -1),
        w_mq,
        w_mk,
        w_mv,
        w_out,
    )


def solution(mesh):
    placed = (
        P(("groups", "tm"), None),
        P(None, ("groups", "tm")),
        P(("groups", "tm"), None),
        P(("groups", "tm")),
    ) + (P(),) * 8
    return jax.shard_map(
        functools.partial(on_device, mesh.shape["tm"]),
        mesh=mesh,
        in_specs=placed,
        out_specs=P(("groups", "tm"), None),
        check_vma=False,
    )
```

```python
import functools

import jax
import jax.numpy as jnp
from jax import lax
from jax.experimental import pallas as pl
from jax.experimental.pallas import tpu as pltpu
from jax.sharding import PartitionSpec as P

H = 8
DK = 64
DV = 128
MH = 4
MD = 128
MC = 512
P_SIZE = 128
BLK = 64
MEM = 8
PLANE = 4
EXTRA = 16
NEG = -1e30
HIGHEST = lax.Precision.HIGHEST
F32 = jnp.float32
BF16 = jnp.bfloat16
NT = (((1,), (1,)), ((), ()))
TN = (((0,), (0,)), ((), ()))


def dot(a, b, dims=(((1,), (0,)), ((), ())), precision=None):
    return lax.dot_general(a, b, dims, precision=precision, preferred_element_type=F32)


def kernel(
    n,
    idx_ref,
    cnt_ref,
    tok_ref,
    ld_ref,
    wrq_hbm,
    wrk_hbm,
    wrv_hbm,
    gain_ref,
    wmq_hbm,
    wmk_hbm,
    wmv_hbm,
    wout_hbm,
    out_ref,
    msg_out,
    msg_in,
    pre_out,
    state_in,
    kv,
    k_s,
    v_s,
    q_s,
    o_s,
    hid_s,
    mq_s,
    sel_s,
    m_s,
    l_s,
    acc_s,
    send1,
    recv1,
    send2,
    recv2,
    send_kv,
    recv_kv,
    wrq_ref,
    wrk_ref,
    wrv_ref,
    wmq_ref,
    wmk_ref,
    wmv_ref,
    wout_ref,
    load_w,
):
    rows = tok_ref.shape[0]
    fpd = rows // P_SIZE
    slice_rows = pre_out.shape[1]
    planes = n // PLANE
    me = lax.axis_index("tm")
    z = me // PLANE
    p = me % PLANE
    core_mate = z * PLANE + (p + 1 - 2 * (p % 2))
    p_y = (p + 2) % PLANE
    y_mate = z * PLANE + p_y

    def load(i, src, dst):
        return pltpu.make_async_copy(src, dst, load_w.at[i])

    load_rk = load(0, wrk_hbm, wrk_ref)
    load_rv = load(1, wrv_hbm, wrv_ref)
    load_rq = load(2, wrq_hbm, wrq_ref)
    load_mk = load(3, wmk_hbm, wmk_ref)
    load_mv = load(4, wmv_hbm, wmv_ref)
    load_mq = load(5, wmq_hbm, wmq_ref)
    load_out = load(6, wout_hbm, wout_ref)
    for copy in (load_rk, load_rv, load_rq, load_mk, load_mv, load_mq, load_out):
        copy.start()

    barrier = pltpu.get_barrier_semaphore()

    def greet(i, carry):
        pl.semaphore_signal(barrier, inc=1, device_id={"tm": (me + i) % n})
        return carry

    lax.fori_loop(1, n, greet, 0)

    tok = tok_ref[...]
    load_rk.wait()
    k_s[...] = dot(tok, wrk_ref[...]).astype(BF16)
    load_rv.wait()
    v_s[...] = dot(tok, wrv_ref[...]).astype(BF16)

    t_id = lax.broadcasted_iota(jnp.int32, (rows, rows), 0)
    s_id = lax.broadcasted_iota(jnp.int32, (rows, rows), 1)
    same = (t_id // BLK) % 2 == (s_id // BLK) % 2
    causal = same & (t_id >= s_id)
    causal_f = jnp.where(causal, 1.0, 0.0).astype(F32)
    same_f = jnp.where(same, 1.0, 0.0).astype(F32)
    ld = ld_ref[...]
    cum_col = dot(causal_f, ld, NT, HIGHEST)
    cum_row = dot(ld, causal_f, NT, HIGHEST)
    total_col = dot(same_f, ld, NT, HIGHEST)
    tail = jnp.exp(total_col - cum_col)
    reach = jnp.exp(cum_col)
    lane = lax.broadcasted_iota(jnp.int32, (rows, 2 * DK), 1)
    chain = (lax.broadcasted_iota(jnp.int32, (rows, 2 * DK), 0) // BLK) % 2
    first_head = lane < DK
    unit_row = lax.broadcasted_iota(jnp.int32, (2 * DK, DV), 0)
    extra_row = lax.broadcasted_iota(jnp.int32, (EXTRA, DV), 0)
    per_unit = DK // slice_rows
    for b in range(2):
        chain_f = jnp.where(chain == b, 1.0, 0.0).astype(F32)
        total = dot(ld, chain_f, precision=HIGHEST)
        for pair in range(H // 2):
            at = pl.ds(pair * 2 * DK, 2 * DK)
            weight = jnp.where(
                first_head, tail[:, 2 * pair : 2 * pair + 1], tail[:, 2 * pair + 1 : 2 * pair + 2]
            )
            scaled = (k_s[:, at].astype(F32) * weight * chain_f).astype(BF16)
            both = dot(scaled, v_s[:, pl.ds(pair * 2 * DV, 2 * DV)], TN)
            state = jnp.where(unit_row < DK, both[:, :DV], both[:, DV:]).astype(BF16)
            for half in range(2):
                head = 2 * pair + half
                d = jnp.broadcast_to(total[head : head + 1, :], (EXTRA, DV))
                hi = d.astype(BF16).astype(F32)
                mid = (d - hi).astype(BF16).astype(F32)
                low = d - hi - mid
                parts = jnp.where(
                    extra_row == 0,
                    hi,
                    jnp.where(extra_row == 1, mid, jnp.where(extra_row == 2, low, 0.0)),
                ).astype(BF16)
                for piece in range(per_unit):
                    j = (b * H + head) * per_unit + piece
                    start = half * DK + piece * slice_rows
                    msg_out[j, pl.ds(0, slice_rows), :] = state[start : start + slice_rows]
                    msg_out[j, pl.ds(slice_rows, EXTRA), :] = parts

    pl.semaphore_wait(barrier, n - 1)

    def copy1(dst, slot):
        return pltpu.make_async_remote_copy(
            src_ref=msg_out.at[dst],
            dst_ref=msg_in.at[slot],
            send_sem=send1.at[dst],
            recv_sem=recv1.at[slot],
            device_id={"tm": dst},
        )

    def send_slices(i, carry):
        copy1((me + i) % n, me).start()
        return carry

    lax.fori_loop(1, n, send_slices, 0)
    msg_in[me] = msg_out[me]

    load_rq.wait()
    q_s[...] = (dot(tok, wrq_ref[...]).astype(BF16).astype(F32) * DK**-0.5).astype(BF16)
    for head in range(H):
        pair = head // 2
        at = pl.ds(pair * 2 * DK, 2 * DK)
        mine = first_head if head % 2 == 0 else jnp.logical_not(first_head)
        qh = jnp.where(mine, q_s[:, at].astype(F32), 0.0).astype(BF16)
        gaps = cum_col[:, head : head + 1] - cum_row[head : head + 1, :]
        decay = jnp.exp(jnp.where(causal, gaps, NEG))
        scores = (dot(qh, k_s[:, at], NT) * decay).astype(BF16)
        o_s[:, pl.ds(head * DV, DV)] = dot(scores, v_s[:, pl.ds(head * DV, DV)])

    def copy2(dst, slot):
        return pltpu.make_async_remote_copy(
            src_ref=pre_out.at[dst],
            dst_ref=state_in.at[slot],
            send_sem=send2.at[dst],
            recv_sem=recv2.at[slot],
            device_id={"tm": dst},
        )

    def hop(i, before):
        @pl.when(i != me)
        def _():
            copy1(i, i).wait_recv()

        pre_out[i] = before.astype(BF16)

        @pl.when(i != me)
        def _():
            copy2(i, me).start()

        d = msg_in[i, pl.ds(slice_rows, EXTRA), :].astype(F32)
        d = d[0:1] + d[1:2] + d[2:3]
        return jnp.exp(d) * before + msg_in[i, pl.ds(0, slice_rows), :].astype(F32)

    lax.fori_loop(0, n, hop, jnp.zeros((slice_rows, DV), F32))
    state_in[me] = pre_out[me]

    def take(i, carry):
        copy2((me + i) % n, (me + n - i) % n).wait_recv()
        return carry

    lax.fori_loop(1, n, take, 0)

    half_units = n // 2
    pair_slices = 2 * per_unit
    for head in range(H):
        pair = head // 2
        at = pl.ds(pair * 2 * DK, 2 * DK)
        mine = first_head if head % 2 == 0 else jnp.logical_not(first_head)
        qh = jnp.where(mine, q_s[:, at].astype(F32) * reach[:, head : head + 1], 0.0)
        col = pl.ds(head * DV, DV)
        o = o_s[:, col]
        for b in range(2):
            incoming = state_in[pl.ds(b * half_units + pair * pair_slices, pair_slices)]
            incoming = incoming.reshape(2 * DK, DV)
            o = o + dot(jnp.where(chain == b, qh, 0.0).astype(BF16), incoming)
        scale = lax.rsqrt(jnp.mean(o * o, axis=-1, keepdims=True) + 1e-05)
        y = o * scale * gain_ref[:, col]
        hid_s[:, col] = (tok_ref[:, col].astype(F32) + y).astype(BF16)

    half_rows = rows // 2

    def copy_kv(slot, half, role, dst):
        part = kv.at[slot, pl.ds(half * half_rows, half_rows), :]
        return pltpu.make_async_remote_copy(
            src_ref=part,
            dst_ref=part,
            send_sem=send_kv.at[role, slot, half],
            recv_sem=recv_kv.at[slot, half],
            device_id={"tm": dst},
        )

    up = (me + PLANE) % n
    not_top = z < planes - 1
    crossing = z * PLANE + p_y

    def pass_on(slot, half):
        @pl.when(not_top)
        def _():
            copy_kv(slot, half, 0, up).start()

        copy_kv(slot, half, 1, core_mate).start()

    load_mk.wait()
    load_mv.wait()
    for half in range(2):
        part = pl.ds(half * half_rows, half_rows)
        kv[me, part, pl.ds(0, MC)] = dot(hid_s[part, :], wmk_ref[...]).astype(BF16)
        kv[me, part, pl.ds(MC, MC)] = dot(hid_s[part, :], wmv_ref[...]).astype(BF16)
        copy_kv(me, half, 2, y_mate).start()
        pass_on(me, half)

    load_mq.wait()
    mq_s[...] = dot(hid_s[...], wmq_ref[...]).astype(BF16)
    key_scale = MD**-0.5
    own_frame = (t_id // P_SIZE) == (s_id // P_SIZE)
    for h in range(MH):
        col = pl.ds(h * MD, MD)
        s = dot(mq_s[:, col], kv[me, :, pl.ds(h * MD, MD)], NT) * key_scale
        s = jnp.where(own_frame, s, NEG)
        m = jnp.max(s, axis=-1, keepdims=True)
        e = jnp.exp(s - m)
        m_s[h] = jnp.broadcast_to(m, (rows, 128))
        l_s[h] = jnp.broadcast_to(jnp.sum(e, axis=-1, keepdims=True), (rows, 128))
        acc_s[:, col] = dot(e.astype(BF16), kv[me, :, pl.ds(MC + h * MD, MD)])

    def attend(owners):
        keys = len(owners) * P_SIZE
        slot = lax.broadcasted_iota(jnp.int32, (P_SIZE, keys), 1) // P_SIZE
        key_owner = jnp.full((P_SIZE, keys), owners[0], jnp.int32)
        for w in range(1, len(owners)):
            key_owner = jnp.where(slot == w, owners[w], key_owner)
        live = []
        wants = [jnp.int32(0)] * len(owners)
        for f in range(fpd):
            hit = jnp.full((P_SIZE, keys), NEG, F32)
            count = cnt_ref[f]
            for i in range(MEM):
                frame = idx_ref[f, i]
                owner = jnp.where(i < count, lax.div(frame, jnp.int32(fpd)), -1)
                local = lax.rem(frame, jnp.int32(fpd))
                hit = jnp.where(key_owner == owner, 0.0, hit)
                wants = [
                    jnp.where(owner == owners[w], local, wants[w]) for w in range(len(owners))
                ]
            live.append(hit)
        bias = jnp.concatenate(live, axis=0)
        for w in range(len(owners)):
            chosen = kv[owners[w], pl.ds(0, P_SIZE), :]
            want = jnp.full((P_SIZE, 2 * MC), wants[w], jnp.int32)
            for f in range(1, fpd):
                chosen = jnp.where(want == f, kv[owners[w], pl.ds(f * P_SIZE, P_SIZE), :], chosen)
            sel_s[pl.ds(w * P_SIZE, P_SIZE), :] = chosen
        for h in range(MH):
            col = pl.ds(h * MD, MD)
            s = dot(mq_s[:, col], sel_s[pl.ds(0, keys), pl.ds(h * MD, MD)], NT) * key_scale + bias
            m_old = m_s[h][:, 0:1]
            m = jnp.maximum(m_old, jnp.max(s, axis=-1, keepdims=True))
            fade = jnp.exp(m_old - m)
            e = jnp.exp(s - m)
            m_s[h] = jnp.broadcast_to(m, (rows, 128))
            l_new = l_s[h][:, 0:1] * fade + jnp.sum(e, axis=-1, keepdims=True)
            l_s[h] = jnp.broadcast_to(l_new, (rows, 128))
            acc_s[:, col] = acc_s[:, col] * fade + dot(
                e.astype(BF16), sel_s[pl.ds(0, keys), pl.ds(MC + h * MD, MD)]
            )

    p_near = p + 1 - 2 * (p % 2)
    p_diagonal = p_y + 1 - 2 * (p_y % 2)

    def wait_core(slot):
        for half in range(2):
            copy_kv(slot, half, 1, core_mate).wait_recv()

    def plane_step(j, carry):
        base = (z - j) * PLANE

        @pl.when(j != 1)
        def _():
            copy_kv(base + p_y, 0, 2, y_mate).wait_recv()
            copy_kv(base + p_y, 0, 1, core_mate).start()

        @pl.when(j < z)
        def _():
            below = base - PLANE + p
            copy_kv(below, 0, 0, up).wait_recv()
            pass_on(below, 0)

            @pl.when(j > 0)
            def _():
                copy_kv(below, 0, 2, y_mate).start()

        copy_kv(base + p_y, 1, 2, y_mate).wait_recv()
        copy_kv(base + p_y, 1, 1, core_mate).start()

        @pl.when(j < z)
        def _():
            below = base - PLANE + p
            copy_kv(below, 1, 0, up).wait_recv()
            copy_kv(below, 1, 2, y_mate).start()
            pass_on(below, 1)

        @pl.when(jnp.logical_and(j == z, not_top))
        def _():
            copy_kv(crossing, 0, 0, up).start()

        wait_core(base + p_near)

        @pl.when(j != 1)
        def _():
            wait_core(base + p_diagonal)
            attend([base + w for w in range(PLANE)])

        @pl.when(j == 1)
        def _():
            attend([base + p, base + p_near])

        return carry

    lax.fori_loop(0, z + 1, plane_step, 0)

    @pl.when(z > 0)
    def _():
        base = (z - 1) * PLANE
        copy_kv(base + p_y, 0, 0, up).wait_recv()
        copy_kv(base + p_y, 0, 1, core_mate).start()
        wait_core(base + p_diagonal)
        attend([base + p_y, base + p_diagonal])

    for h in range(MH):
        col = pl.ds(h * MD, MD)
        mq_s[:, col] = (acc_s[:, col] / l_s[h][:, 0:1]).astype(BF16)
    load_out.wait()
    projected = dot(mq_s[...], wout_ref[...])
    out_ref[...] = (hid_s[...].astype(F32) + projected).astype(BF16)

    def drain(i, carry):
        dst = (me + i) % n
        copy1(dst, me).wait_send()
        copy2(dst, me).wait_send()
        return carry

    lax.fori_loop(1, n, drain, 0)

    def drain_kv(j, carry):
        base = (z - j) * PLANE
        for half in range(2):

            @pl.when(not_top)
            def _():
                copy_kv(base + p, half, 0, up).wait_send()

            copy_kv(base + p, half, 1, core_mate).wait_send()
            copy_kv(base + p_y, half, 1, core_mate).wait_send()

        @pl.when(j != 1)
        def _():
            copy_kv(base + p, 0, 2, y_mate).wait_send()

        copy_kv(base + p, 1, 2, y_mate).wait_send()
        return carry

    lax.fori_loop(0, z + 1, drain_kv, 0)

    @pl.when(not_top)
    def _():
        copy_kv(crossing, 0, 0, up).wait_send()


def on_device(
    n, tokens, log_decay, mem_index, mem_count, w_rq, w_rk, w_rv, norm_gain, w_mq, w_mk, w_mv, w_out
):
    rows, width = tokens.shape
    slice_rows = 2 * H * DK // n
    vmem = pl.BlockSpec(memory_space=pltpu.VMEM)
    smem = pl.BlockSpec(memory_space=pltpu.SMEM)
    hbm = pl.BlockSpec(memory_space=pl.ANY)
    weights = (w_rq, w_rk, w_rv, w_mq, w_mk, w_mv, w_out)
    return pl.pallas_call(
        functools.partial(kernel, n),
        out_shape=jax.ShapeDtypeStruct((rows, width), BF16),
        in_specs=[smem, smem, vmem, vmem] + [hbm] * 3 + [vmem] + [hbm] * 4,
        out_specs=vmem,
        scratch_shapes=[
            pltpu.VMEM((n, slice_rows + EXTRA, DV), BF16),
            pltpu.VMEM((n, slice_rows + EXTRA, DV), BF16),
            pltpu.VMEM((n, slice_rows, DV), BF16),
            pltpu.VMEM((n, slice_rows, DV), BF16),
            pltpu.VMEM((n, rows, 2 * MC), BF16),
            pltpu.VMEM((rows, H * DK), BF16),
            pltpu.VMEM((rows, H * DV), BF16),
            pltpu.VMEM((rows, H * DK), BF16),
            pltpu.VMEM((rows, H * DV), F32),
            pltpu.VMEM((rows, width), BF16),
            pltpu.VMEM((rows, MC), BF16),
            pltpu.VMEM((PLANE * P_SIZE, 2 * MC), BF16),
            pltpu.VMEM((MH, rows, 128), F32),
            pltpu.VMEM((MH, rows, 128), F32),
            pltpu.VMEM((rows, MC), F32),
            pltpu.SemaphoreType.DMA((n,)),
            pltpu.SemaphoreType.DMA((n,)),
            pltpu.SemaphoreType.DMA((n,)),
            pltpu.SemaphoreType.DMA((n,)),
            pltpu.SemaphoreType.DMA((3, n, 2)),
            pltpu.SemaphoreType.DMA((n, 2)),
        ]
        + [pltpu.VMEM(w.shape, BF16) for w in weights]
        + [pltpu.SemaphoreType.DMA((len(weights),))],
        compiler_params=pltpu.CompilerParams(
            collective_id=0, has_side_effects=True, vmem_limit_bytes=56 * 2**20
        ),
    )(
        mem_index,
        mem_count,
        tokens,
        log_decay,
        w_rq,
        w_rk,
        w_rv,
        norm_gain.reshape(1, -1),
        w_mq,
        w_mk,
        w_mv,
        w_out,
    )


def solution(mesh):
    placed = (
        P(("groups", "tm"), None),
        P(None, ("groups", "tm")),
        P(("groups", "tm"), None),
        P(("groups", "tm")),
    ) + (P(),) * 8
    return jax.shard_map(
        functools.partial(on_device, mesh.shape["tm"]),
        mesh=mesh,
        in_specs=placed,
        out_specs=P(("groups", "tm"), None),
        check_vma=False,
    )
```
